256 devices in a mesh: branch: 2 (over y_lo), seq: 8 (over x, y_hi), dp: 16 (over z, core).
Axes of the slice: x: 4, y: 4 (y_hi: 2, y_lo: 2; y = y_hi * 2 + y_lo), z: 8, core: 2. Of those that a mesh axis runs over, the one named last changes fastest.
Arguments:
- query_rows: bfloat16 [2, 16, 1024, 3072], P('branch', 'dp', 'seq'), may hold values from -64 to 64
- key_rows: bfloat16 [2, 16, 1024, 3072], P('branch', 'dp', 'seq'), may hold values from -8 to 8
- value_rows: bfloat16 [2, 16, 1024, 3072], P('branch', 'dp', 'seq'), may hold values from -6 to 6
- cotangent: bfloat16 [2, 16, 1024, 3072], P('branch', 'dp', 'seq'), may hold values from -6 to 6
- proj_weight: bfloat16 [2, 3072, 3072], P('branch', ('seq', 'dp')), may hold values from -0.4375 to 0.4375
- time_weight: bfloat16 [2, 256, 3072], P('branch'), may hold values from -0.375 to 0.375
- timestep: int32 [16], P('dp'), may hold values from 0 to 999
- text_count: int32 [16], P('dp'), may hold values from 64 to 256
Outputs:
- block_out: bfloat16 [2, 16, 1024, 3072], P('branch', 'dp', 'seq')
- query_grad: bfloat16 [2, 16, 1024, 3072], P('branch', 'dp', 'seq')
- key_grad: bfloat16 [2, 16, 1024, 3072], P('branch', 'dp', 'seq')
- value_grad: bfloat16 [2, 16, 1024, 3072], P('branch', 'dp', 'seq')
- proj_grad: float32 [2, 3072, 3072], P('branch', ('seq', 'dp'))
The draws below stay inside these ranges and needn't reach their ends.
All inputs are finite; a program needn't handle non-finite values.
Results may differ from the reference program's by a relative error of at most 0.022.
Values may be sent and summed in bfloat16 or wider, within the bound.
A program may use at most 128 MiB of HBM per device.

```python
import math
from functools import partial
import jax
import jax.numpy as jnp
from jax import lax

HEADS = 24
HEAD_DIM = 128
D = 3072
FREQ = 256
GROUPS = 8
LENGTH = 1024
TEXT = 256
SAMPLES = 16


def shared_base(key):
    raw_normal = jax.random.normal(jax.random.fold_in(key, 101), (2, SAMPLES, LENGTH, D), jnp.float32)
    return jnp.clip(raw_normal, -6.0, 6.0)


def draw_key_rows(key, part):
    base_keys = shared_base(key)
    result_keys = base_keys
    return result_keys.astype(jnp.bfloat16)


def draw_query_rows(key, part):
    key = jax.random.fold_in(key, 5)
    own_normal = jnp.clip(jax.random.normal(key, (2, SAMPLES, LENGTH, D), jnp.float32), -6.0, 6.0)
    result_queries = 2.0 * own_normal
    return result_queries.astype(jnp.bfloat16)


def touch_ends(drawn, own_key, low, largest):
    longest = drawn.shape.index(max(drawn.shape))
    spots = []
    for shift in (0, 1):
        where = [jax.random.randint(jax.random.fold_in(own_key, axis), (), 0, length) for axis, length in enumerate(drawn.shape)]
        where[longest] = (where[longest] + shift) % drawn.shape[longest]
        spots.append(tuple(where))
    return drawn.at[spots[0]].set(low).at[spots[1]].set(largest)


def shard_levels(rng, shape, shards, smallest, largest):
    def one(axis_at, parts):
        steps = jax.random.uniform(jax.random.fold_in(jax.random.fold_in(rng, 6), axis_at), (parts,), jnp.float32, smallest / len(shards), largest / len(shards))
        return jnp.repeat(jnp.exp(steps), shape[axis_at] // parts).reshape((-1,) + (1,) * (len(shape) - axis_at - 1))

    gain = one(*shards[0])
    for cut in shards[1:]:
        gain = gain * one(*cut)
    return gain


def gaussian(own_key, dims, width, bound, split=(), kind=jnp.bfloat16):
    array = width * jax.random.normal(own_key, dims, jnp.float32)
    if split:
        array = array * shard_levels(own_key, dims, split, -0.22, 0.18)
    return jnp.clip(array, -bound, bound).astype(kind)


def setup_inputs(seed: int = 0) -> dict:
    key_of = jax.random.split(jax.random.key(seed), 9)
    query_rows = draw_query_rows(jax.random.fold_in(key_of[8], 71), 0)
    key_rows = draw_key_rows(jax.random.fold_in(key_of[8], 71), 0)
    value_rows = gaussian(key_of[2], (2, SAMPLES, LENGTH, D), 1.0, 6.0, ((0, 2), (1, 16), (2, 8)))
    cotangent = gaussian(key_of[3], (2, SAMPLES, LENGTH, D), 1.0, 6.0, ((0, 2), (1, 16), (2, 8)))
    proj_weight = gaussian(key_of[4], (2, D, D), (D // 16) ** -0.5, 0.4375, ((0, 2), (1, 128)))
    time_weight = gaussian(key_of[5], (2, FREQ, D), FREQ ** -0.5, 0.375, ((0, 2),))
    timestep = touch_ends(jax.random.randint(key_of[6], (SAMPLES,), 0, 1000), jax.random.fold_in(key_of[6], 1), 0, 999).astype(jnp.int32)
    text_count = touch_ends(jax.random.randint(key_of[7], (SAMPLES,), TEXT // 4, TEXT + 1), jax.random.fold_in(key_of[7], 1), TEXT // 4, TEXT).astype(jnp.int32)
    return dict(query_rows=query_rows, key_rows=key_rows, value_rows=value_rows, cotangent=cotangent, proj_weight=proj_weight, time_weight=time_weight, timestep=timestep, text_count=text_count)


def time_features(step_value, feature_count):
    half_count = feature_count // 2
    frequency = jnp.exp(-math.log(10000.0) * jnp.arange(half_count, dtype=jnp.float32) / half_count)
    phases = step_value.astype(jnp.float32) * frequency
    raw_features = jnp.concatenate([jnp.cos(phases), jnp.sin(phases)])
    return jax.nn.silu(raw_features).astype(jnp.bfloat16)


def key_allowed(length, text_limit):
    positions = jnp.arange(length)
    return jnp.logical_or(positions >= length // 4, positions < text_limit)


def masked_softmax(scores, allowed):
    masked = jnp.where(allowed[None, None, :], scores, -jnp.inf)
    highest = jnp.max(masked, axis=-1, keepdims=True)
    exponent = jnp.exp(masked - highest)
    return exponent / jnp.sum(exponent, axis=-1, keepdims=True)


def heads_forward(queries, key_heads, value_heads, allowed):
    length, head_count, head_width = queries.shape
    block_rows = min(512, length)
    scaling = head_width ** -0.5
    key_float = key_heads.astype(jnp.float32)
    value_float = value_heads.astype(jnp.float32)
    blocks = queries.reshape(length // block_rows, block_rows, head_count, head_width)

    def single(query_block):
        scores = jnp.einsum("qhe,khe->hqk", query_block.astype(jnp.float32), key_float) * scaling
        attn_probs = masked_softmax(scores, allowed).astype(jnp.bfloat16)
        mixed_rows = jnp.einsum("hqk,khe->qhe", attn_probs.astype(jnp.float32), value_float)
        return mixed_rows.astype(jnp.bfloat16)

    return lax.map(single, blocks).reshape(length, head_count * head_width)


def heads_backward(queries, key_heads, value_heads, grad_heads, allowed):
    length, head_count, head_width = queries.shape
    block_rows = min(512, length)
    block_count = length // block_rows
    scaling = head_width ** -0.5
    key_float = key_heads.astype(jnp.float32)
    value_float = value_heads.astype(jnp.float32)
    query_blocks = queries.reshape(block_count, block_rows, head_count, head_width)
    grad_blocks = grad_heads.reshape(block_count, block_rows, head_count, head_width)

    def advance(running, block_pair):
        key_acc, value_acc = running
        query_block, grad_block = block_pair
        query_float = query_block.astype(jnp.float32)
        grad_float = grad_block.astype(jnp.float32)
        scores = jnp.einsum("qhe,khe->hqk", query_float, key_float) * scaling
        attn_probs = masked_softmax(scores, allowed)
        prob_grad = jnp.einsum("qhe,khe->hqk", grad_float, value_float)
        score_grad = attn_probs * (prob_grad - jnp.sum(attn_probs * prob_grad, axis=-1, keepdims=True))
        score_float = score_grad.astype(jnp.bfloat16).astype(jnp.float32)
        query_part = (jnp.einsum("hqk,khe->qhe", score_float, key_float) * scaling).astype(jnp.bfloat16)
        key_acc = key_acc + jnp.einsum("hqk,qhe->khe", score_float, query_float)
        probs_float = attn_probs.astype(jnp.bfloat16).astype(jnp.float32)
        value_acc = value_acc + jnp.einsum("hqk,qhe->khe", probs_float, grad_float)
        return (key_acc, value_acc), query_part

    zero_heads = jnp.zeros((length, head_count, head_width), jnp.float32)
    (key_acc, value_acc), query_parts = lax.scan(advance, (zero_heads, zero_heads), (query_blocks, grad_blocks))
    flat_width = head_count * head_width
    query_part = query_parts.reshape(length, flat_width)
    key_part = (key_acc * scaling).astype(jnp.bfloat16).reshape(length, flat_width)
    value_part = value_acc.astype(jnp.bfloat16).reshape(length, flat_width)
    return query_part, key_part, value_part


def reference(query_rows, key_rows, value_rows, cotangent, proj_weight, time_weight, timestep, text_count):
    group_heads = HEADS // GROUPS
    group_width = group_heads * HEAD_DIM
    features = jax.vmap(partial(time_features, feature_count=FREQ))(timestep)
    gate = jnp.einsum("sf,bfd->bsd", features.astype(jnp.float32), time_weight.astype(jnp.float32))
    allowed = jax.vmap(partial(key_allowed, LENGTH))(text_count)

    def split_groups(rows_in):
        return rows_in.reshape(LENGTH, GROUPS, group_heads, HEAD_DIM).transpose(1, 0, 2, 3)

    def merge_groups(grouped):
        return grouped.transpose(1, 0, 2).reshape(LENGTH, D)

    branch_sums = []
    branch_attended = []
    for branch in range(2):
        weight_groups = proj_weight[branch].reshape(GROUPS, group_width, D)

        def sample_forward(sample_item):
            query_all, key_all, value_all, gate_row, allowed_row = sample_item

            def group_step(running_sum, group_parts):
                query_grp, key_grp, value_grp, weight_grp = group_parts
                attended_grp = heads_forward(query_grp, key_grp, value_grp, allowed_row)
                partial_grp = (jnp.dot(attended_grp, weight_grp, preferred_element_type=jnp.float32) * gate_row).astype(jnp.bfloat16)
                return running_sum + partial_grp.astype(jnp.float32), attended_grp

            start_sum = jnp.zeros((LENGTH, D), jnp.float32)
            return lax.scan(group_step, start_sum, (split_groups(query_all), split_groups(key_all), split_groups(value_all), weight_groups))

        sum_rows, attended_rows = lax.map(sample_forward, (query_rows[branch], key_rows[branch], value_rows[branch], gate[branch], allowed))
        branch_sums.append(sum_rows)
        branch_attended.append(attended_rows)

    block_out = jnp.stack([branch_sums[0] + branch_sums[1], branch_sums[1]]).astype(jnp.bfloat16)
    base_grad = cotangent[0].astype(jnp.float32)
    out_grad = jnp.stack([base_grad, base_grad + cotangent[1].astype(jnp.float32)])
    scaled_grad = (out_grad * gate[:, :, None, :]).astype(jnp.bfloat16)

    query_grads = []
    key_grads = []
    value_grads = []
    proj_grads = []
    for branch in range(2):
        weight_groups = proj_weight[branch].reshape(GROUPS, group_width, D)

        def sample_backward(running_sum, sample_item):
            query_all, key_all, value_all, scaled_row, attended_row, allowed_row = sample_item

            def group_step(unused, group_parts):
                query_grp, key_grp, value_grp, weight_grp, attended_grp = group_parts
                attended_grad = jnp.dot(scaled_row, weight_grp.T, preferred_element_type=jnp.float32).astype(jnp.bfloat16)
                weight_part = jnp.dot(attended_grp.T, scaled_row, preferred_element_type=jnp.float32)
                grad_heads = attended_grad.reshape(LENGTH, group_heads, HEAD_DIM)
                query_part, key_part, value_part = heads_backward(query_grp, key_grp, value_grp, grad_heads, allowed_row)
                return unused, (weight_part, query_part, key_part, value_part)

            unused, group_outs = lax.scan(group_step, jnp.zeros((), jnp.float32), (split_groups(query_all), split_groups(key_all), split_groups(value_all), weight_groups, attended_row))
            weight_parts, query_parts, key_parts, value_parts = group_outs
            new_sum = running_sum + weight_parts.reshape(D, D)
            return new_sum, (merge_groups(query_parts), merge_groups(key_parts), merge_groups(value_parts))

        start_sum = jnp.zeros((D, D), jnp.float32)
        grad_sum, grad_rows = lax.scan(sample_backward, start_sum, (query_rows[branch], key_rows[branch], value_rows[branch], scaled_grad[branch], branch_attended[branch], allowed))
        if branch == 0:
            proj_grads.append(jnp.zeros((D, D), jnp.float32))
        else:
            proj_grads.append(grad_sum / SAMPLES)
        query_grads.append(grad_rows[0])
        key_grads.append(grad_rows[1])
        value_grads.append(grad_rows[2])

    return (block_out, jnp.stack(query_grads), jnp.stack(key_grads), jnp.stack(value_grads), jnp.stack(proj_grads))
```

```python
import functools
import math

import jax
import jax.numpy as jnp
from jax import lax
from jax.experimental import pallas as pl
from jax.experimental.pallas import tpu as pltpu
from jax.sharding import PartitionSpec as P

HEAD_DIM = 128
TOK = 128
SEQ = 8
WIDTH = 3072
GROUP = 384
HEADS = 3
LENGTH = 1024
TEXT = 256
HALF = 1536
UNIT = 48
ROWS = 24
MESH = pl.DeviceIdType.MESH
F32 = jnp.float32
BF16 = jnp.bfloat16
SCALE = HEAD_DIM ** (-0.5)
TO_EXP2 = SCALE * math.log2(math.e)
COPIES = 63 + 63 + 64


def dot(a, b):
    return jnp.dot(a, b, preferred_element_type=F32)


def dot_rows(a, b):
    return lax.dot_general(a, b, (((1,), (1,)), ((), ())), preferred_element_type=F32)


def kernel(
    q_in, k_in, v_in, cot_in, w_in, gate_in, bias_in,
    out, dq, dk, dv, wg,
    q_h, k_h, v_h, exps, o_f, l_inv, att, att2, g_tok, g_h, ag, gs_buf, ds_buf,
    dq_h, dk_h, dv_h, w_own, w_rx, w_all, cot_rx, part, rs_rx, out_tx, out_rx,
    wg_own, wg_tx, wg_rx, wg_z, wg_zrx, wg_acc, wg_yrx, wg_tot, wg_crx,
    send_sem, recv_sem, local_sem,
):
    b = lax.axis_index("branch")
    s = lax.axis_index("seq")
    d = lax.axis_index("dp")
    x, h = lax.div(s, 2), lax.rem(s, 2)
    z, c = lax.div(d, 2), lax.rem(d, 2)
    seq_peer = [(b, lax.rem(s + k, SEQ), d) for k in range(SEQ)]
    z_peer = [(b, s, lax.rem(d + 2 * k, 16)) for k in range(8)]
    y_peer = (b, s + 1 - 2 * h, d)
    core_peer = (b, s, d + 1 - 2 * c)
    branch_peer = (1 - b, s, d)

    used = [0, 0]

    def remote(src, dst, device):
        i = used[0]
        used[0] += 1
        return pltpu.make_async_remote_copy(
            src_ref=src, dst_ref=dst, send_sem=send_sem.at[i], recv_sem=recv_sem.at[i],
            device_id=device, device_id_type=MESH,
        )

    def local(src, dst):
        i = used[1]
        used[1] += 1
        return pltpu.make_async_copy(src, dst, local_sem.at[i])

    barrier = pltpu.get_barrier_semaphore()
    everyone = seq_peer[1:] + z_peer[1:] + [core_peer, branch_peer]
    for device in everyone:
        pl.semaphore_signal(barrier, inc=1, device_id=device, device_id_type=MESH)
    w_own[...] = w_in[...].astype(F32)
    v_h[:, :, HEAD_DIM:] = jnp.ones((HEADS, LENGTH, HEAD_DIM), BF16)
    pl.semaphore_wait(barrier, len(everyone))

    def lanes(index, size):
        return pl.ds(pl.multiple_of(index * size, size), size)

    own_half = lanes(c, HALF)
    other_half = lanes(1 - c, HALF)
    unit_rows = pl.ds(pl.multiple_of(z * UNIT, 16), UNIT)

    w_copy = remote(w_own.at[:, other_half], w_rx, core_peer)
    w_copy.start()
    cot_copy = remote(cot_in, cot_rx, branch_peer)

    @pl.when(b == 0)
    def _():
        cot_copy.start()

    in_copies = []
    for j in range(HEADS):
        head_copies = []
        for src, dst, wide in ((q_in, q_h, False), (k_in, k_h, False), (v_in, v_h, True)):
            def place(owner):
                rows = lanes(owner, TOK)
                if wide:
                    return dst.at[j, rows, pl.ds(0, HEAD_DIM)]
                return dst.at[j, rows, :]
            for k in range(SEQ):
                peer = seq_peer[k][1]
                cols = pl.ds(pl.multiple_of(peer * GROUP + j * HEAD_DIM, HEAD_DIM), HEAD_DIM)
                if k == 0:
                    copy = local(src.at[:, cols], place(s))
                else:
                    copy = remote(src.at[:, cols], place(s), seq_peer[k])
                copy.start()
                head_copies.append(copy)
        in_copies.append(head_copies)

    w_copy.wait()
    first = c == 0
    own_part = w_own[:, own_half]
    other_part = w_rx[...]
    w_all[h, unit_rows, own_half] = jnp.concatenate(
        [jnp.where(first, own_part, other_part), jnp.where(first, other_part, own_part)], axis=0
    ).astype(BF16)
    w_y = remote(w_all.at[h, unit_rows, own_half], w_all.at[h, unit_rows, own_half], y_peer)
    w_y.start()
    w_y.wait()
    w_z = []
    for k in range(1, 8):
        piece = w_all.at[:, unit_rows, own_half]
        copy = remote(piece, piece, z_peer[k])
        copy.start()
        w_z.append(copy)

    def forward_head(j):
        for n, copy in enumerate(in_copies[j]):
            if n % SEQ == 0:
                copy.wait()
            else:
                copy.wait_recv()

        def step(i, carry):
            rows = pl.ds(pl.multiple_of(i * 256, 256), 256)
            queries = q_h[j, rows, :]
            text = dot_rows(queries, k_h[j, :TEXT, :]) + bias_in[...]
            image = dot_rows(queries, k_h[j, TEXT:, :])
            highest = jnp.maximum(
                jnp.max(text, axis=1, keepdims=True), jnp.max(image, axis=1, keepdims=True)
            )
            text = jnp.exp2((text - highest) * TO_EXP2).astype(BF16)
            image = jnp.exp2((image - highest) * TO_EXP2).astype(BF16)
            exps[j, rows, :TEXT] = text
            exps[j, rows, TEXT:] = image
            mixed = dot(text, v_h[j, :TEXT, :]) + dot(image, v_h[j, TEXT:, :])
            inverse = 1.0 / mixed[:, HEAD_DIM:]
            result = mixed[:, :HEAD_DIM] * inverse
            l_inv[j, rows, :] = inverse
            o_f[j, rows, :] = result
            result = result.astype(BF16)
            cols = slice(j * HEAD_DIM, (j + 1) * HEAD_DIM)
            att[i, 0, :, cols] = result[:TOK]
            att[i, 1, :, cols] = result[TOK:]
            return carry

        lax.fori_loop(0, 4, step, 0)
        cols = pl.ds(j * HEAD_DIM, HEAD_DIM)
        away = remote(att.at[:, 1 - h, :, cols], att2.at[h, :, :, cols], y_peer)
        away.start()
        here = local(att.at[:, h, :, cols], att2.at[h, :, :, cols])
        here.start()
        return away, here

    att_copies = [forward_head(0)]

    @pl.when(b == 0)
    def _():
        g_tok[x] = (cot_in[...].astype(F32) * gate_in[...]).astype(BF16)

    @pl.when(b == 1)
    def _():
        cot_copy.wait_recv()
        g_tok[x] = (
            (cot_in[...].astype(F32) + cot_rx[...].astype(F32)) * gate_in[...]
        ).astype(BF16)

    g_copies = []
    for i in (1, 3, 2):
        copy = remote(g_tok.at[x], g_tok.at[x], seq_peer[2 * i])
        copy.start()
        g_copies.append(copy)

    att_copies.append(forward_head(1))
    for copy in w_z:
        copy.wait_recv()
    w_swap = remote(w_all.at[:, :, own_half], w_all.at[:, :, own_half], core_peer)
    w_swap.start()
    att_copies.append(forward_head(2))
    w_swap.wait_recv()
    for away, here in att_copies:
        away.wait_recv()
        here.wait()

    rs_copies = []
    for n in range(3):
        def project(m, carry):
            cols = pl.ds(pl.multiple_of(n * 1024 + m * 512, 512), 512)
            rows0 = att2[0].reshape(512, GROUP)
            rows1 = att2[1].reshape(512, GROUP)
            summed = dot(rows0, w_all[0, :, cols]) + dot(rows1, w_all[1, :, cols])
            gated = (summed * gate_in[:, cols]).astype(BF16)
            part[:, :, cols] = gated.reshape(4, TOK, 512)
            return carry

        lax.fori_loop(0, 2, project, 0)
        cols = pl.ds(n * 1024, 1024)
        for i in (1, 3, 2):
            target = lax.rem(x + i, 4)
            copy = remote(part.at[target, :, cols], rs_rx.at[i, :, cols], seq_peer[2 * i])
            copy.start()
            rs_copies.append(copy)

    for copy in g_copies:
        copy.wait_recv()

    def attended_grad(group):
        def step(i, carry):
            rows = g_tok[pl.ds(i * 2, 2)].reshape(256, WIDTH)
            grads = dot_rows(rows, w_all[group]).astype(BF16)
            ag[group, pl.ds(i * 2, 2)] = grads.reshape(2, TOK, GROUP)
            return carry

        lax.fori_loop(0, 2, step, 0)

    attended_grad(1 - h)
    grad_away = remote(ag.at[1 - h], g_h.at[:, h], y_peer)
    grad_away.start()
    attended_grad(h)
    grad_here = local(ag.at[h], g_h.at[:, h])
    grad_here.start()

    wg_swap = remote(wg_tx, wg_rx, core_peer)

    def weight_products(half, store):
        for group in range(2):
            turned = jnp.transpose(att2[group].reshape(512, GROUP))

            def step(m, carry):
                source = pl.ds(pl.multiple_of(half * HALF + m * 512, 512), 512)
                cols = pl.ds(pl.multiple_of(m * 512, 512), 512)
                store(group, cols, dot(turned, g_tok[:, :, source].reshape(512, 512)))
                return carry

            lax.fori_loop(0, 3, step, 0)

    @pl.when(b == 1)
    def _():
        def store_tx(group, cols, value):
            wg_tx[group, :, cols] = value.astype(BF16)

        def store_own(group, cols, value):
            wg_own[group, :, cols] = value

        weight_products(1 - c, store_tx)
        wg_swap.start()
        weight_products(c, store_own)

    grad_away.wait_recv()
    grad_here.wait()

    back = []

    def backward_head(j):
        cols = slice(j * HEAD_DIM, (j + 1) * HEAD_DIM)

        def step(i, carry):
            rows = pl.ds(pl.multiple_of(i * 256, 256), 256)
            grads = g_h[i, :, :, cols].reshape(256, HEAD_DIM).astype(F32)
            scaled = (grads * l_inv[j, rows, :]).astype(BF16)
            gs_buf[rows, :] = scaled
            shift = jnp.sum(scaled.astype(F32) * o_f[j, rows, :], axis=1, keepdims=True)
            prob_grad = dot_rows(scaled, v_h[j, :, :HEAD_DIM])
            score = (exps[j, rows, :].astype(F32) * (prob_grad - shift)).astype(BF16)
            ds_buf[rows, :] = score
            dq_h[j, rows, :] = (dot(score, k_h[j]) * SCALE).astype(BF16)
            return carry

        lax.fori_loop(0, 4, step, 0)
        q_turned = jnp.transpose(q_h[j])
        g_turned = jnp.transpose(gs_buf[...])

        def keys(i, carry):
            rows = pl.ds(pl.multiple_of(i * 256, 256), 256)
            key_part = dot(q_turned, ds_buf[:, rows])
            dk_h[j, rows, :] = (jnp.transpose(key_part) * SCALE).astype(BF16)
            value_part = dot(g_turned, exps[j, :, rows])
            dv_h[j, rows, :] = jnp.transpose(value_part).astype(BF16)
            return carry

        lax.fori_loop(0, 4, keys, 0)
        for src, dst in ((dq_h, dq), (dk_h, dk), (dv_h, dv)):
            own_cols = pl.ds(pl.multiple_of(s * GROUP + j * HEAD_DIM, HEAD_DIM), HEAD_DIM)
            for k in range(SEQ):
                piece = src.at[j, lanes(seq_peer[k][1], TOK), :]
                if k == 0:
                    copy = local(piece, dst.at[:, own_cols])
                else:
                    copy = remote(piece, dst.at[:, own_cols], seq_peer[k])
                copy.start()
                back.append((k, copy))

    backward_head(0)

    wg_zs = [
        remote(
            wg_z.at[:, pl.ds(pl.multiple_of(lax.rem(z + k, 8) * UNIT, 16), UNIT), :],
            wg_zrx.at[k],
            z_peer[k],
        )
        for k in range(1, 8)
    ]

    @pl.when(b == 1)
    def _():
        wg_swap.wait_recv()
        wg_z[...] = (wg_own[...] + wg_rx[...].astype(F32)).astype(BF16)
        for copy in wg_zs:
            copy.start()

    for copy in rs_copies:
        copy.wait_recv()
    out_copy = remote(out_tx, out_rx, branch_peer)
    total = part[x].astype(F32)
    for i in (1, 2, 3):
        total += rs_rx[i].astype(F32)

    @pl.when(b == 1)
    def _():
        rounded = total.astype(BF16)
        out_tx[...] = rounded
        out[...] = rounded
        out_copy.start()

    backward_head(1)
    backward_head(2)

    @pl.when(b == 0)
    def _():
        out_copy.wait_recv()
        again = part[x].astype(F32)
        for i in (1, 2, 3):
            again += rs_rx[i].astype(F32)
        out[...] = (again + out_rx[...].astype(F32)).astype(BF16)
        wg[...] = jnp.zeros((ROWS, WIDTH), F32)
        cot_copy.wait_send()

    wg_y = remote(wg_acc.at[1 - h], wg_yrx, y_peer)
    wg_c = remote(wg_tot.at[pl.ds(pl.multiple_of((1 - c) * ROWS, 8), ROWS), :], wg_crx, core_peer)

    @pl.when(b == 1)
    def _():
        for copy in wg_zs:
            copy.wait_recv()
        summed = wg_z[:, unit_rows, :].astype(F32)
        for k in range(1, 8):
            summed += wg_zrx[k].astype(F32)
        wg_acc[...] = summed * (1.0 / 16.0)
        wg_y.start()
        wg_y.wait_recv()
        wg_tot[...] = wg_acc[h] + wg_yrx[...]
        wg_c.start()
        wg[:, own_half] = wg_tot[pl.ds(pl.multiple_of(c * ROWS, 8), ROWS), :]
        wg_c.wait_recv()
        wg[:, other_half] = wg_crx[...]
        wg_c.wait_send()
        wg_y.wait_send()
        wg_swap.wait_send()
        out_copy.wait_send()
        for copy in wg_zs:
            copy.wait_send()

    for k, copy in back:
        if k == 0:
            copy.wait()
        else:
            copy.wait_recv()
    for head_copies in in_copies:
        for k, copy in enumerate(head_copies):
            if k % SEQ:
                copy.wait_send()
    for copy in w_z + [w_swap] + [away for away, here in att_copies] + g_copies + rs_copies:
        copy.wait_send()
    grad_away.wait_send()
    for k, copy in back:
        if k:
            copy.wait_send()


def vmem(shape, dtype=BF16):
    return pltpu.VMEM(shape, dtype)


def time_features(step_value, feature_count):
    half_count = feature_count // 2
    frequency = jnp.exp(-math.log(10000.0) * jnp.arange(half_count, dtype=F32) / half_count)
    phases = step_value.astype(F32) * frequency
    raw_features = jnp.concatenate([jnp.cos(phases), jnp.sin(phases)])
    return jax.nn.silu(raw_features).astype(BF16)


def shards(
    query_rows, key_rows, value_rows, cotangent, proj_weight, time_weight, timestep, text_count
):
    features = time_features(timestep[0], time_weight.shape[1])
    gate_row = jnp.dot(features[None, :], time_weight[0], preferred_element_type=F32)
    bias = jnp.where(jnp.arange(TEXT) < text_count[0], 0.0, -jnp.inf).astype(F32)[None, :]
    any_spec = pl.BlockSpec(memory_space=pl.ANY)
    vmem_spec = pl.BlockSpec(memory_space=pltpu.VMEM)
    rows_shape = jax.ShapeDtypeStruct((TOK, WIDTH), BF16)
    scratch = [
        vmem((HEADS, LENGTH, HEAD_DIM)), vmem((HEADS, LENGTH, HEAD_DIM)),
        vmem((HEADS, LENGTH, 2 * HEAD_DIM)),
        vmem((HEADS, LENGTH, LENGTH)),
        vmem((HEADS, LENGTH, HEAD_DIM), F32), vmem((HEADS, LENGTH, HEAD_DIM), F32),
        vmem((4, 2, TOK, GROUP)), vmem((2, 4, TOK, GROUP)),
        vmem((4, TOK, WIDTH)), vmem((4, 2, TOK, GROUP)), vmem((2, 4, TOK, GROUP)),
        vmem((LENGTH, HEAD_DIM)), vmem((LENGTH, LENGTH)),
        vmem((HEADS, LENGTH, HEAD_DIM)), vmem((HEADS, LENGTH, HEAD_DIM)),
        vmem((HEADS, LENGTH, HEAD_DIM)),
        vmem((ROWS, WIDTH), F32), vmem((ROWS, HALF), F32), vmem((2, GROUP, WIDTH)),
        vmem((TOK, WIDTH)), vmem((4, TOK, WIDTH)), vmem((4, TOK, WIDTH)),
        vmem((TOK, WIDTH)), vmem((TOK, WIDTH)),
        vmem((2, GROUP, HALF), F32), vmem((2, GROUP, HALF)), vmem((2, GROUP, HALF)),
        vmem((2, GROUP, HALF)), vmem((8, 2, UNIT, HALF)),
        vmem((2, UNIT, HALF), F32), vmem((UNIT, HALF), F32), vmem((UNIT, HALF), F32),
        vmem((ROWS, HALF), F32),
        pltpu.SemaphoreType.DMA((COPIES,)), pltpu.SemaphoreType.DMA((COPIES,)),
        pltpu.SemaphoreType.DMA((32,)),
    ]
    block_out, dq, dk, dv, wg = pl.pallas_call(
        kernel,
        out_shape=(rows_shape, rows_shape, rows_shape, rows_shape,
                   jax.ShapeDtypeStruct((ROWS, WIDTH), F32)),
        in_specs=[any_spec] * 3 + [vmem_spec] * 4,
        out_specs=(vmem_spec, any_spec, any_spec, any_spec, vmem_spec),
        scratch_shapes=scratch,
        compiler_params=pltpu.CompilerParams(
            collective_id=0, has_side_effects=True, vmem_limit_bytes=60 * 2**20
        ),
        cost_estimate=pl.CostEstimate(
            flops=14 * 10**9, bytes_accessed=8 * 10**6, transcendentals=3 * 2**20
        ),
        name="block",
    )(query_rows[0, 0], key_rows[0, 0], value_rows[0, 0], cotangent[0, 0], proj_weight[0],
      gate_row, bias)
    return (block_out[None, None], dq[None, None], dk[None, None], dv[None, None], wg[None])


def solution(mesh):
    rows = P("branch", "dp", "seq", None)
    weight = P("branch", ("seq", "dp"), None)
    return jax.shard_map(
        shards,
        mesh=mesh,
        in_specs=(rows, rows, rows, rows, weight, P("branch", None, None), P("dp"), P("dp")),
        out_specs=(rows, rows, rows, rows, weight),
        check_vma=False,
    )
```

```python
import functools
import math

import jax
import jax.numpy as jnp
from jax import lax
from jax.experimental import pallas as pl
from jax.experimental.pallas import tpu as pltpu
from jax.sharding import PartitionSpec as P

HEAD_DIM = 128
TOK = 128
SEQ = 8
WIDTH = 3072
GROUP = 384
HEADS = 3
LENGTH = 1024
TEXT = 256
HALF = 1536
UNIT = 48
ROWS = 24
MESH = pl.DeviceIdType.MESH
F32 = jnp.float32
BF16 = jnp.bfloat16
SCALE = HEAD_DIM ** (-0.5)
TO_EXP2 = SCALE * math.log2(math.e)
COPIES = 192


def dot(a, b):
    return jnp.dot(a, b, preferred_element_type=F32)


def dot_rows(a, b):
    return lax.dot_general(a, b, (((1,), (1,)), ((), ())), preferred_element_type=F32)


class Transfers:
    def __init__(self, branch, send_sem, recv_sem, local_sem):
        self.branch, self.sems, self.local_sem = branch, (send_sem, recv_sem), local_sem
        self.remotes, self.locals = 0, 0
        self.sends, self.recvs = [], []

    def on(self, side, action):
        if side is None:
            action()
        else:
            pl.when(self.branch == side)(action)

    def remote(self, src, dst, device, sender=None, receiver=None):
        i = self.remotes
        self.remotes += 1
        copy = pltpu.make_async_remote_copy(
            src_ref=src, dst_ref=dst, send_sem=self.sems[0].at[i], recv_sem=self.sems[1].at[i],
            device_id=device, device_id_type=MESH,
        )
        self.on(sender, copy.start)
        self.sends.append((copy, sender))
        self.recvs.append((copy, receiver, True))
        return copy

    def local(self, src, dst):
        i = self.locals
        self.locals += 1
        copy = pltpu.make_async_copy(src, dst, self.local_sem.at[i])
        copy.start()
        self.recvs.append((copy, None, False))
        return copy

    def arrive(self, *copies):
        for copy in copies:
            entry = next(e for e in self.recvs if e[0] is copy)
            self.recvs = [e for e in self.recvs if e is not entry]
            self.on(entry[1], copy.wait_recv if entry[2] else copy.wait)

    def sent(self, copy):
        entry = next(e for e in self.sends if e[0] is copy)
        self.sends = [e for e in self.sends if e is not entry]
        self.on(entry[1], copy.wait_send)

    def finish(self):
        self.arrive(*[entry[0] for entry in self.recvs])
        for copy, side in self.sends:
            self.on(side, copy.wait_send)


def kernel(
    q_in, k_in, v_in, cot_in, w_in, gate_in, bias_in,
    out, dq, dk, dv, wg,
    q_h, k_h, v_h, exps, o_f, l_inv, att, att2, g_tok, g_h, ag, gs_buf, ds_buf,
    dq_h, dk_h, dv_h, w_own, w_rx, w_all, cot_rx, part, rs_relay, rs_rx, out_tx, out_rx,
    wg_own, wg_tx, wg_rx, wg_z, wg_zrx, wg_acc, wg_yrx, wg_tot, wg_crx,
    send_sem, recv_sem, local_sem,
):
    b = lax.axis_index("branch")
    s = lax.axis_index("seq")
    d = lax.axis_index("dp")
    x, h = lax.div(s, 2), lax.rem(s, 2)
    z, c = lax.div(d, 2), lax.rem(d, 2)
    seq_peer = [(b, lax.rem(s + k, SEQ), d) for k in range(SEQ)]
    z_peer = [(b, s, lax.rem(d + 2 * k, 16)) for k in range(8)]
    x_right, x_left = seq_peer[2], seq_peer[6]
    z_right, z_left = z_peer[1], z_peer[7]
    y_peer = (b, s + 1 - 2 * h, d)
    core_peer = (b, s, d + 1 - 2 * c)
    branch_peer = (1 - b, s, d)
    moves = Transfers(b, send_sem, recv_sem, local_sem)

    barrier = pltpu.get_barrier_semaphore()
    everyone = seq_peer[1:] + z_peer[1:] + [core_peer, branch_peer]
    for device in everyone:
        pl.semaphore_signal(barrier, inc=1, device_id=device, device_id_type=MESH)
    w_own[...] = w_in[...].astype(F32)
    v_h[:, :, HEAD_DIM:] = jnp.ones((HEADS, LENGTH, HEAD_DIM), BF16)
    pl.semaphore_wait(barrier, len(everyone))

    def lanes(index, size):
        return pl.ds(pl.multiple_of(index * size, size), size)

    own_half = lanes(c, HALF)
    other_half = lanes(1 - c, HALF)

    def unit(k):
        return pl.ds(pl.multiple_of(lax.rem(z + k + 8, 8) * UNIT, 16), UNIT)

    w_copy = moves.remote(w_own.at[:, other_half], w_rx, core_peer)
    cot_copy = moves.remote(cot_in, cot_rx, branch_peer, sender=0, receiver=1)

    def send_in(j, offsets):
        copies = []
        for src, dst, wide in ((q_in, q_h, False), (k_in, k_h, False), (v_in, v_h, True)):
            here = dst.at[j, lanes(s, TOK), pl.ds(0, HEAD_DIM)] if wide else dst.at[j, lanes(s, TOK), :]
            for k in offsets:
                peer = seq_peer[k][1]
                cols = pl.ds(pl.multiple_of(peer * GROUP + j * HEAD_DIM, HEAD_DIM), HEAD_DIM)
                if k == 0:
                    copies.append(moves.local(src.at[:, cols], here))
                else:
                    copies.append(moves.remote(src.at[:, cols], here, seq_peer[k]))
        return copies

    moves.arrive(w_copy)
    first = c == 0
    own_part = w_own[:, own_half]
    other_part = w_rx[...]
    w_all[h, unit(0), own_half] = jnp.concatenate(
        [jnp.where(first, own_part, other_part), jnp.where(first, other_part, own_part)], axis=0
    ).astype(BF16)
    w_y = moves.remote(w_all.at[h, unit(0), own_half], w_all.at[h, unit(0), own_half], y_peer)
    in_copies = [send_in(j, (0, 2, 6, 4)) for j in range(HEADS)]
    moves.arrive(w_y)
    w_swaps = []

    def w_swap(k):
        piece = w_all.at[:, unit(k), own_half]
        w_swaps.append(moves.remote(piece, piece, core_peer))

    def w_send(k, peer):
        piece = w_all.at[:, unit(k), own_half]
        return moves.remote(piece, piece, peer)

    w_moves = [w_send(0, z_right), w_send(0, z_left)]
    w_swap(0)

    moves.sent(cot_copy)

    @pl.when(b == 0)
    def _():
        g_tok[x] = (cot_in[...].astype(F32) * gate_in[...]).astype(BF16)

    moves.arrive(cot_copy)

    @pl.when(b == 1)
    def _():
        g_tok[x] = (
            (cot_in[...].astype(F32) + cot_rx[...].astype(F32)) * gate_in[...]
        ).astype(BF16)

    top, low = pl.ds(0, 64), pl.ds(64, 64)

    def g_send(block, rows, peer):
        piece = g_tok.at[lax.rem(x + block, 4), rows]
        return moves.remote(piece, piece, peer)

    g_first = [g_send(0, top, x_right), g_send(0, low, x_left)]
    for j in range(HEADS):
        in_copies[j] += send_in(j, (1, 7, 3, 5))
        if j == 0:
            g_rest = [g_send(0, low, x_right), g_send(0, top, x_left)]

    def w_step(t):
        nonlocal w_moves
        moves.arrive(*w_moves)
        if t < 3:
            w_moves = [w_send(-t, z_right), w_send(t, z_left)]
        elif t == 3:
            low = w_all.at[0, unit(-3), own_half]
            high = w_all.at[1, unit(3), own_half]
            w_moves = [moves.remote(low, low, z_right), moves.remote(high, high, z_left)]
        if t < 4:
            w_swap(-t)
            w_swap(t)
        else:
            w_swap(4)

    def forward_head(j):
        moves.arrive(*in_copies[j])
        cols = slice(j * HEAD_DIM, (j + 1) * HEAD_DIM)
        for i in range(4):
            rows = pl.ds(i * 256, 256)
            queries = q_h[j, rows, :]
            text = dot_rows(queries, k_h[j, :TEXT, :]) + bias_in[...]
            image = dot_rows(queries, k_h[j, TEXT:, :])
            highest = jnp.maximum(
                jnp.max(text, axis=1, keepdims=True), jnp.max(image, axis=1, keepdims=True)
            )
            text = jnp.exp2((text - highest) * TO_EXP2).astype(BF16)
            image = jnp.exp2((image - highest) * TO_EXP2).astype(BF16)
            exps[j, rows, :TEXT] = text
            exps[j, rows, TEXT:] = image
            mixed = dot(text, v_h[j, :TEXT, :]) + dot(image, v_h[j, TEXT:, :])
            inverse = 1.0 / mixed[:, HEAD_DIM:]
            result = mixed[:, :HEAD_DIM] * inverse
            l_inv[j, rows, :] = inverse
            o_f[j, rows, :] = result
            result = result.astype(BF16)
            att[i, 0, :, cols] = result[:TOK]
            att[i, 1, :, cols] = result[TOK:]
        cols = pl.ds(j * HEAD_DIM, HEAD_DIM)
        return [
            moves.remote(att.at[:, 1 - h, :, cols], att2.at[h, :, :, cols], y_peer),
            moves.local(att.at[:, h, :, cols], att2.at[h, :, :, cols]),
        ]

    w_step(1)
    att_copies = forward_head(0)
    w_step(2)
    att_copies += forward_head(1)
    w_step(3)
    moves.arrive(*g_first)
    g_far = [g_send(3, top, x_right), g_send(1, low, x_left)]
    att_copies += forward_head(2)
    w_step(4)
    moves.arrive(*w_swaps)
    moves.arrive(*att_copies)

    far, right, left = lax.rem(x + 2, 4), lax.rem(x + 1, 4), lax.rem(x + 3, 4)
    relays = []
    for n in range(3):
        cols = pl.ds(n * 1024, 1024)
        for m in range(2):
            at = pl.ds(n * 1024 + m * 512, 512)
            rows0 = att2[0].reshape(512, GROUP)
            rows1 = att2[1].reshape(512, GROUP)
            summed = dot(rows0, w_all[0, :, at]) + dot(rows1, w_all[1, :, at])
            part[:, :, at] = (summed * gate_in[:, at]).astype(BF16).reshape(4, TOK, 512)
        relays.append([
            moves.remote(part.at[far, top, cols], rs_relay.at[0, :, cols], x_right),
            moves.remote(part.at[far, low, cols], rs_relay.at[1, :, cols], x_left),
        ])

    moves.arrive(*g_rest)
    moves.arrive(*g_far)

    def attended_grad(group, i):
        rows = g_tok[pl.ds(i * 2, 2)].reshape(256, WIDTH)
        grads = dot_rows(rows, w_all[group]).astype(BF16)
        ag[group, pl.ds(i * 2, 2)] = grads.reshape(2, TOK, GROUP)

    grad_copies = [[], []]
    for i in range(2):
        attended_grad(1 - h, i)
        pair = pl.ds(i * 2, 2)
        grad_copies[i].append(moves.remote(ag.at[1 - h, pair], g_h.at[pair, h], y_peer))
    for i in range(2):
        attended_grad(h, i)
        pair = pl.ds(i * 2, 2)
        grad_copies[i].append(moves.local(ag.at[h, pair], g_h.at[pair, h]))

    rs_copies = []
    for n in range(3):
        cols = pl.ds(n * 1024, 1024)
        moves.arrive(*relays[n])
        part[right, top, cols] = (
            part[right, top, cols].astype(F32) + rs_relay[0, :, cols].astype(F32)
        ).astype(BF16)
        part[left, low, cols] = (
            part[left, low, cols].astype(F32) + rs_relay[1, :, cols].astype(F32)
        ).astype(BF16)
        rs_copies += [
            moves.remote(part.at[right, :, cols], rs_rx.at[0, :, cols], x_right),
            moves.remote(part.at[left, :, cols], rs_rx.at[1, :, cols], x_left),
        ]

    def weight_products(half, store):
        for group in range(2):
            turned = jnp.transpose(att2[group].reshape(512, GROUP))

            def step(m, carry):
                source = pl.ds(pl.multiple_of(half * HALF + m * 512, 512), 512)
                cols = pl.ds(pl.multiple_of(m * 512, 512), 512)
                store(group, cols, dot(turned, g_tok[:, :, source].reshape(512, 512)))
                return carry

            lax.fori_loop(0, 3, step, 0)

    def store_tx(group, cols, value):
        wg_tx[group, :, cols] = value.astype(BF16)

    def store_own(group, cols, value):
        wg_own[group, :, cols] = value

    pl.when(b == 1)(lambda: weight_products(1 - c, store_tx))
    wg_swap = moves.remote(wg_tx, wg_rx, core_peer, sender=1, receiver=1)
    pl.when(b == 1)(lambda: weight_products(c, store_own))

    def backward_head(j):
        cols = slice(j * HEAD_DIM, (j + 1) * HEAD_DIM)
        for i in range(4):
            if j == 0 and i % 2 == 0:
                moves.arrive(*grad_copies[i // 2])
            rows = pl.ds(i * 256, 256)
            grads = g_h[i, :, :, cols].reshape(256, HEAD_DIM).astype(F32)
            scaled = (grads * l_inv[j, rows, :]).astype(BF16)
            gs_buf[rows, :] = scaled
            shift = jnp.sum(scaled.astype(F32) * o_f[j, rows, :], axis=1, keepdims=True)
            prob_grad = dot_rows(scaled, v_h[j, :, :HEAD_DIM])
            score = (exps[j, rows, :].astype(F32) * (prob_grad - shift)).astype(BF16)
            ds_buf[rows, :] = score
            dq_h[j, rows, :] = (dot(score, k_h[j]) * SCALE).astype(BF16)
        q_turned = jnp.transpose(q_h[j])
        g_turned = jnp.transpose(gs_buf[...])
        for i in range(4):
            rows = pl.ds(i * 256, 256)
            key_part = dot(q_turned, ds_buf[:, rows])
            dk_h[j, rows, :] = (jnp.transpose(key_part) * SCALE).astype(BF16)
            value_part = dot(g_turned, exps[j, :, rows])
            dv_h[j, rows, :] = jnp.transpose(value_part).astype(BF16)
        own_cols = pl.ds(pl.multiple_of(s * GROUP + j * HEAD_DIM, HEAD_DIM), HEAD_DIM)
        for src, dst in ((dq_h, dq), (dk_h, dk), (dv_h, dv)):
            for k in range(SEQ):
                piece = src.at[j, lanes(seq_peer[k][1], TOK), :]
                if k == 0:
                    moves.local(piece, dst.at[:, own_cols])
                else:
                    moves.remote(piece, dst.at[:, own_cols], seq_peer[k])

    backward_head(0)

    moves.arrive(wg_swap)

    @pl.when(b == 1)
    def _():
        wg_z[...] = (wg_own[...] + wg_rx[...].astype(F32)).astype(BF16)

    def z_send(slot, group, k_right, k_left):
        return [
            moves.remote(wg_z.at[group[0], unit(k_right), :], wg_zrx.at[0, slot, group[0]], z_right, 1, 1),
            moves.remote(wg_z.at[group[1], unit(k_left), :], wg_zrx.at[1, slot, group[1]], z_left, 1, 1),
        ]

    both = pl.ds(0, 2)
    z_moves = z_send(0, (0, 1), 4, 4)

    def z_step(t):
        nonlocal z_moves
        moves.arrive(*z_moves)
        groups = (0, 1) if t == 1 else (both, both)

        @pl.when(b == 1)
        def _():
            for way, at in ((0, unit(4 - t)), (1, unit(4 + t))):
                wg_z[groups[way], at, :] = (
                    wg_z[groups[way], at, :].astype(F32) + wg_zrx[way, t - 1, groups[way]].astype(F32)
                ).astype(BF16)

        z_moves = z_send(t, (both, both), 4 - t, 4 + t)

    backward_head(1)
    z_step(1)
    backward_head(2)

    moves.arrive(*rs_copies)

    def own_rows():
        return part[x].astype(F32) + rs_rx[0].astype(F32) + rs_rx[1].astype(F32)

    @pl.when(b == 1)
    def _():
        rounded = own_rows().astype(BF16)
        out_tx[...] = rounded
        out[...] = rounded

    out_copy = moves.remote(out_tx, out_rx, branch_peer, sender=1, receiver=0)
    z_step(2)
    z_step(3)
    moves.arrive(*z_moves)

    @pl.when(b == 1)
    def _():
        summed = wg_z[:, unit(0), :].astype(F32)
        summed += wg_zrx[0, 3].astype(F32) + wg_zrx[1, 3].astype(F32)
        wg_acc[...] = summed * (1.0 / 16.0)

    wg_y = moves.remote(wg_acc.at[1 - h], wg_yrx, y_peer, sender=1, receiver=1)
    moves.arrive(wg_y)

    @pl.when(b == 1)
    def _():
        wg_tot[...] = wg_acc[h] + wg_yrx[...]

    away = pl.ds(pl.multiple_of((1 - c) * ROWS, 8), ROWS)
    wg_c = moves.remote(wg_tot.at[away, :], wg_crx, core_peer, sender=1, receiver=1)
    moves.arrive(wg_c)

    @pl.when(b == 1)
    def _():
        wg[:, own_half] = wg_tot[pl.ds(pl.multiple_of(c * ROWS, 8), ROWS), :]
        wg[:, other_half] = wg_crx[...]

    moves.arrive(out_copy)

    @pl.when(b == 0)
    def _():
        out[...] = (own_rows() + out_rx[...].astype(F32)).astype(BF16)
        wg[...] = jnp.zeros((ROWS, WIDTH), F32)

    moves.finish()


def vmem(shape, dtype=BF16):
    return pltpu.VMEM(shape, dtype)


def time_features(step_value, feature_count):
    half_count = feature_count // 2
    frequency = jnp.exp(-math.log(10000.0) * jnp.arange(half_count, dtype=F32) / half_count)
    phases = step_value.astype(F32) * frequency
    raw_features = jnp.concatenate([jnp.cos(phases), jnp.sin(phases)])
    return jax.nn.silu(raw_features).astype(BF16)


def shards(
    query_rows, key_rows, value_rows, cotangent, proj_weight, time_weight, timestep, text_count
):
    features = time_features(timestep[0], time_weight.shape[1])
    gate_row = jnp.dot(features[None, :], time_weight[0], preferred_element_type=F32)
    bias = jnp.where(jnp.arange(TEXT) < text_count[0], 0.0, -jnp.inf).astype(F32)[None, :]
    any_spec = pl.BlockSpec(memory_space=pl.ANY)
    vmem_spec = pl.BlockSpec(memory_space=pltpu.VMEM)
    rows_shape = jax.ShapeDtypeStruct((TOK, WIDTH), BF16)
    scratch = [
        vmem((HEADS, LENGTH, HEAD_DIM)), vmem((HEADS, LENGTH, HEAD_DIM)),
        vmem((HEADS, LENGTH, 2 * HEAD_DIM)),
        vmem((HEADS, LENGTH, LENGTH)),
        vmem((HEADS, LENGTH, HEAD_DIM), F32), vmem((HEADS, LENGTH, HEAD_DIM), F32),
        vmem((4, 2, TOK, GROUP)), vmem((2, 4, TOK, GROUP)),
        vmem((4, TOK, WIDTH)), vmem((4, 2, TOK, GROUP)), vmem((2, 4, TOK, GROUP)),
        vmem((LENGTH, HEAD_DIM)), vmem((LENGTH, LENGTH)),
        vmem((HEADS, LENGTH, HEAD_DIM)), vmem((HEADS, LENGTH, HEAD_DIM)),
        vmem((HEADS, LENGTH, HEAD_DIM)),
        vmem((ROWS, WIDTH), F32), vmem((ROWS, HALF), F32), vmem((2, GROUP, WIDTH)),
        vmem((TOK, WIDTH)), vmem((4, TOK, WIDTH)), vmem((2, 64, WIDTH)), vmem((2, TOK, WIDTH)),
        vmem((TOK, WIDTH)), vmem((TOK, WIDTH)),
        vmem((2, GROUP, HALF), F32), vmem((2, GROUP, HALF)), vmem((2, GROUP, HALF)),
        vmem((2, GROUP, HALF)), vmem((2, 4, 2, UNIT, HALF)),
        vmem((2, UNIT, HALF), F32), vmem((UNIT, HALF), F32), vmem((UNIT, HALF), F32),
        vmem((ROWS, HALF), F32),
        pltpu.SemaphoreType.DMA((COPIES,)), pltpu.SemaphoreType.DMA((COPIES,)),
        pltpu.SemaphoreType.DMA((32,)),
    ]
    block_out, dq, dk, dv, wg = pl.pallas_call(
        kernel,
        out_shape=(rows_shape, rows_shape, rows_shape, rows_shape,
                   jax.ShapeDtypeStruct((ROWS, WIDTH), F32)),
        in_specs=[any_spec] * 3 + [vmem_spec] * 4,
        out_specs=(vmem_spec, any_spec, any_spec, any_spec, vmem_spec),
        scratch_shapes=scratch,
        compiler_params=pltpu.CompilerParams(
            collective_id=0, has_side_effects=True, vmem_limit_bytes=60 * 2**20
        ),
        cost_estimate=pl.CostEstimate(
            flops=14 * 10**9, bytes_accessed=8 * 10**6, transcendentals=3 * 2**20
        ),
        name="block",
    )(query_rows[0, 0], key_rows[0, 0], value_rows[0, 0], cotangent[0, 0], proj_weight[0],
      gate_row, bias)
    return (block_out[None, None], dq[None, None], dk[None, None], dv[None, None], wg[None])


def solution(mesh):
    rows = P("branch", "dp", "seq", None)
    weight = P("branch", ("seq", "dp"), None)
    return jax.shard_map(
        shards,
        mesh=mesh,
        in_specs=(rows, rows, rows, rows, weight, P("branch", None, None), P("dp"), P("dp")),
        out_specs=(rows, rows, rows, rows, weight),
        check_vma=False,
    )
```

```python
import functools
import math

import jax
import jax.numpy as jnp
from jax import lax
from jax.experimental import pallas as pl
from jax.experimental.pallas import tpu as pltpu
from jax.sharding import PartitionSpec as P

HEAD_DIM = 128
TOK = 128
SEQ = 8
WIDTH = 3072
GROUP = 384
HEADS = 3
LENGTH = 1024
TEXT = 256
HALF = 1536
UNIT = 48
ROWS = 24
MESH = pl.DeviceIdType.MESH
F32 = jnp.float32
BF16 = jnp.bfloat16
SCALE = HEAD_DIM ** (-0.5)
TO_EXP2 = SCALE * math.log2(math.e)
COPIES = 192


def dot(a, b):
    return jnp.dot(a, b, preferred_element_type=F32)


def dot_rows(a, b):
    return lax.dot_general(a, b, (((1,), (1,)), ((), ())), preferred_element_type=F32)


class Transfers:
    def __init__(self, branch, send_sem, recv_sem, local_sem):
        self.branch, self.sems, self.local_sem = branch, (send_sem, recv_sem), local_sem
        self.remotes, self.locals = 0, 0
        self.sends, self.recvs = [], []

    def on(self, side, action):
        if side is None:
            action()
        else:
            pl.when(self.branch == side)(action)

    def remote(self, src, dst, device, sender=None, receiver=None):
        i = self.remotes
        self.remotes += 1
        copy = pltpu.make_async_remote_copy(
            src_ref=src, dst_ref=dst, send_sem=self.sems[0].at[i], recv_sem=self.sems[1].at[i],
            device_id=device, device_id_type=MESH,
        )
        self.on(sender, copy.start)
        self.sends.append((copy, sender))
        self.recvs.append((copy, receiver, True))
        return copy

    def local(self, src, dst):
        i = self.locals
        self.locals += 1
        copy = pltpu.make_async_copy(src, dst, self.local_sem.at[i])
        copy.start()
        self.recvs.append((copy, None, False))
        return copy

    def arrive(self, *copies):
        for copy in copies:
            entry = next(e for e in self.recvs if e[0] is copy)
            self.recvs = [e for e in self.recvs if e is not entry]
            self.on(entry[1], copy.wait_recv if entry[2] else copy.wait)

    def sent(self, copy):
        entry = next(e for e in self.sends if e[0] is copy)
        self.sends = [e for e in self.sends if e is not entry]
        self.on(entry[1], copy.wait_send)

    def finish(self):
        self.arrive(*[entry[0] for entry in self.recvs])
        for copy, side in self.sends:
            self.on(side, copy.wait_send)


def kernel(
    q_in, k_in, v_in, cot_in, w_in, gate_in, bias_in,
    out, dq, dk, dv, wg,
    q_h, k_h, v_h, exps, o_f, l_inv, att, att2, g_tok, g_h, ag, gs_buf, ds_buf,
    dq_h, dk_h, dv_h, w_own, w_rx, w_all, cot_rx, part, rs_relay, rs_rx, out_tx, out_rx,
    wg_own, wg_tx, wg_rx, wg_z, wg_zrx, wg_acc, wg_yrx, wg_tot, wg_crx,
    send_sem, recv_sem, local_sem,
):
    b = lax.axis_index("branch")
    s = lax.axis_index("seq")
    d = lax.axis_index("dp")
    x, h = lax.div(s, 2), lax.rem(s, 2)
    z, c = lax.div(d, 2), lax.rem(d, 2)
    seq_peer = [(b, lax.rem(s + k, SEQ), d) for k in range(SEQ)]
    z_peer = [(b, s, lax.rem(d + 2 * k, 16)) for k in range(8)]
    x_right, x_left = seq_peer[2], seq_peer[6]
    z_right, z_left = z_peer[1], z_peer[7]
    y_peer = (b, s + 1 - 2 * h, d)
    core_peer = (b, s, d + 1 - 2 * c)
    branch_peer = (1 - b, s, d)
    moves = Transfers(b, send_sem, recv_sem, local_sem)

    barrier = pltpu.get_barrier_semaphore()
    everyone = seq_peer[1:] + z_peer[1:] + [core_peer, branch_peer]
    for device in everyone:
        pl.semaphore_signal(barrier, inc=1, device_id=device, device_id_type=MESH)
    w_own[...] = w_in[...].astype(F32)
    v_h[:, :, HEAD_DIM:] = jnp.ones((HEADS, LENGTH, HEAD_DIM), BF16)
    pl.semaphore_wait(barrier, len(everyone))

    def lanes(index, size):
        return pl.ds(pl.multiple_of(index * size, size), size)

    own_half = lanes(c, HALF)
    other_half = lanes(1 - c, HALF)

    def unit(k):
        return pl.ds(pl.multiple_of(lax.rem(z + k + 8, 8) * UNIT, 16), UNIT)

    w_copy = moves.remote(w_own.at[:, other_half], w_rx, core_peer)
    top, low = pl.ds(0, 64), pl.ds(64, 64)
    cot_copies = [
        moves.remote(cot_in.at[rows], cot_rx.at[rows], branch_peer, sender=0, receiver=1)
        for rows in (top, low)
    ]

    def send_in(j, offsets):
        copies = []
        for src, dst, wide in ((q_in, q_h, False), (k_in, k_h, False), (v_in, v_h, True)):
            here = dst.at[j, lanes(s, TOK), pl.ds(0, HEAD_DIM)] if wide else dst.at[j, lanes(s, TOK), :]
            for k in offsets:
                peer = seq_peer[k][1]
                cols = pl.ds(pl.multiple_of(peer * GROUP + j * HEAD_DIM, HEAD_DIM), HEAD_DIM)
                if k == 0:
                    copies.append(moves.local(src.at[:, cols], here))
                else:
                    copies.append(moves.remote(src.at[:, cols], here, seq_peer[k]))
        return copies

    moves.arrive(w_copy)
    first = c == 0
    own_part = w_own[:, own_half]
    other_part = w_rx[...]
    w_all[h, unit(0), own_half] = jnp.concatenate(
        [jnp.where(first, own_part, other_part), jnp.where(first, other_part, own_part)], axis=0
    ).astype(BF16)
    w_y = moves.remote(w_all.at[h, unit(0), own_half], w_all.at[h, unit(0), own_half], y_peer)
    in_copies = [send_in(j, (0, 2, 6, 4)) for j in range(HEADS)]
    moves.arrive(w_y)
    w_swaps = []

    def w_swap(k):
        piece = w_all.at[:, unit(k), own_half]
        w_swaps.append(moves.remote(piece, piece, core_peer))

    def w_send(k, peer):
        piece = w_all.at[:, unit(k), own_half]
        return moves.remote(piece, piece, peer)

    w_moves = [w_send(0, z_right), w_send(0, z_left)]
    w_swap(0)

    def w_step(t):
        nonlocal w_moves
        moves.arrive(*w_moves)
        if t < 3:
            w_moves = [w_send(-t, z_right), w_send(t, z_left)]
        elif t == 3:
            low = w_all.at[0, unit(-3), own_half]
            high = w_all.at[1, unit(3), own_half]
            w_moves = [moves.remote(low, low, z_right), moves.remote(high, high, z_left)]
        if t < 4:
            w_swap(-t)
            w_swap(t)
        else:
            w_swap(4)

    def forward_head(j):
        moves.arrive(*in_copies[j])
        cols = slice(j * HEAD_DIM, (j + 1) * HEAD_DIM)
        for i in range(4):
            rows = pl.ds(i * 256, 256)
            queries = q_h[j, rows, :]
            text = dot_rows(queries, k_h[j, :TEXT, :]) + bias_in[...]
            image = dot_rows(queries, k_h[j, TEXT:, :])
            highest = jnp.maximum(
                jnp.max(text, axis=1, keepdims=True), jnp.max(image, axis=1, keepdims=True)
            )
            text = jnp.exp2((text - highest) * TO_EXP2).astype(BF16)
            image = jnp.exp2((image - highest) * TO_EXP2).astype(BF16)
            exps[j, rows, :TEXT] = text
            exps[j, rows, TEXT:] = image
            mixed = dot(text, v_h[j, :TEXT, :]) + dot(image, v_h[j, TEXT:, :])
            inverse = 1.0 / mixed[:, HEAD_DIM:]
            result = mixed[:, :HEAD_DIM] * inverse
            l_inv[j, rows, :] = inverse
            o_f[j, rows, :] = result
            result = result.astype(BF16)
            att[i, 0, :, cols] = result[:TOK]
            att[i, 1, :, cols] = result[TOK:]
        cols = pl.ds(j * HEAD_DIM, HEAD_DIM)
        return [
            moves.remote(att.at[:, 1 - h, :, cols], att2.at[h, :, :, cols], y_peer),
            moves.local(att.at[:, h, :, cols], att2.at[h, :, :, cols]),
        ]

    def gate_rows(rows):
        @pl.when(b == 0)
        def _():
            g_tok[x, rows] = (cot_in[rows, :].astype(F32) * gate_in[...]).astype(BF16)

        @pl.when(b == 1)
        def _():
            g_tok[x, rows] = (
                (cot_in[rows, :].astype(F32) + cot_rx[rows, :].astype(F32)) * gate_in[...]
            ).astype(BF16)

    def g_send(block, rows, peer):
        piece = g_tok.at[lax.rem(x + block, 4), rows]
        return moves.remote(piece, piece, peer)

    moves.arrive(cot_copies[0])
    gate_rows(top)
    g_first = [g_send(0, top, x_right)]
    g_rest = [g_send(0, top, x_left)]
    w_step(1)
    moves.arrive(cot_copies[1])
    gate_rows(low)
    g_first.append(g_send(0, low, x_left))
    g_rest.append(g_send(0, low, x_right))
    for copy in cot_copies:
        moves.sent(copy)
    for j in range(HEADS):
        in_copies[j] += send_in(j, (1, 7, 3, 5))
    w_step(2)
    w_step(3)
    w_step(4)
    moves.arrive(*g_first)
    g_far = [g_send(3, top, x_right), g_send(1, low, x_left)]
    att_copies = forward_head(0) + forward_head(1) + forward_head(2)
    moves.arrive(*w_swaps)
    moves.arrive(*att_copies)

    far, right, left = lax.rem(x + 2, 4), lax.rem(x + 1, 4), lax.rem(x + 3, 4)
    relays = []
    for n in range(3):
        cols = pl.ds(n * 1024, 1024)
        for m in range(2):
            at = pl.ds(n * 1024 + m * 512, 512)
            rows0 = att2[0].reshape(512, GROUP)
            rows1 = att2[1].reshape(512, GROUP)
            summed = dot(rows0, w_all[0, :, at]) + dot(rows1, w_all[1, :, at])
            part[:, :, at] = (summed * gate_in[:, at]).astype(BF16).reshape(4, TOK, 512)
        relays.append([
            moves.remote(part.at[far, top, cols], rs_relay.at[0, :, cols], x_right),
            moves.remote(part.at[far, low, cols], rs_relay.at[1, :, cols], x_left),
        ])

    moves.arrive(*g_rest)
    moves.arrive(*g_far)

    def attended_grad(group, i):
        rows = g_tok[pl.ds(i * 2, 2)].reshape(256, WIDTH)
        grads = dot_rows(rows, w_all[group]).astype(BF16)
        ag[group, pl.ds(i * 2, 2)] = grads.reshape(2, TOK, GROUP)

    grad_copies = [[], []]
    for i in range(2):
        attended_grad(1 - h, i)
        pair = pl.ds(i * 2, 2)
        grad_copies[i].append(moves.remote(ag.at[1 - h, pair], g_h.at[pair, h], y_peer))
    for i in range(2):
        attended_grad(h, i)
        pair = pl.ds(i * 2, 2)
        grad_copies[i].append(moves.local(ag.at[h, pair], g_h.at[pair, h]))

    rs_copies = []
    for n in range(3):
        cols = pl.ds(n * 1024, 1024)
        moves.arrive(*relays[n])
        part[right, top, cols] = (
            part[right, top, cols].astype(F32) + rs_relay[0, :, cols].astype(F32)
        ).astype(BF16)
        part[left, low, cols] = (
            part[left, low, cols].astype(F32) + rs_relay[1, :, cols].astype(F32)
        ).astype(BF16)
        rs_copies += [
            moves.remote(part.at[right, :, cols], rs_rx.at[0, :, cols], x_right),
            moves.remote(part.at[left, :, cols], rs_rx.at[1, :, cols], x_left),
        ]

    def weight_products(half, store):
        for group in range(2):
            turned = jnp.transpose(att2[group].reshape(512, GROUP))

            def step(m, carry):
                source = pl.ds(pl.multiple_of(half * HALF + m * 512, 512), 512)
                cols = pl.ds(pl.multiple_of(m * 512, 512), 512)
                store(group, cols, dot(turned, g_tok[:, :, source].reshape(512, 512)))
                return carry

            lax.fori_loop(0, 3, step, 0)

    def store_tx(group, cols, value):
        wg_tx[group, :, cols] = value.astype(BF16)

    def store_own(group, cols, value):
        wg_own[group, :, cols] = value

    pl.when(b == 1)(lambda: weight_products(1 - c, store_tx))
    wg_swap = moves.remote(wg_tx, wg_rx, core_peer, sender=1, receiver=1)
    pl.when(b == 1)(lambda: weight_products(c, store_own))

    def backward_head(j):
        cols = slice(j * HEAD_DIM, (j + 1) * HEAD_DIM)
        for i in range(4):
            if j == 0 and i % 2 == 0:
                moves.arrive(*grad_copies[i // 2])
            rows = pl.ds(i * 256, 256)
            grads = g_h[i, :, :, cols].reshape(256, HEAD_DIM).astype(F32)
            scaled = (grads * l_inv[j, rows, :]).astype(BF16)
            gs_buf[rows, :] = scaled
            shift = jnp.sum(scaled.astype(F32) * o_f[j, rows, :], axis=1, keepdims=True)
            prob_grad = dot_rows(scaled, v_h[j, :, :HEAD_DIM])
            score = (exps[j, rows, :].astype(F32) * (prob_grad - shift)).astype(BF16)
            ds_buf[rows, :] = score
            dq_h[j, rows, :] = (dot(score, k_h[j]) * SCALE).astype(BF16)
        q_turned = jnp.transpose(q_h[j])
        g_turned = jnp.transpose(gs_buf[...])
        for i in range(4):
            rows = pl.ds(i * 256, 256)
            key_part = dot(q_turned, ds_buf[:, rows])
            dk_h[j, rows, :] = (jnp.transpose(key_part) * SCALE).astype(BF16)
            value_part = dot(g_turned, exps[j, :, rows])
            dv_h[j, rows, :] = jnp.transpose(value_part).astype(BF16)
        own_cols = pl.ds(pl.multiple_of(s * GROUP + j * HEAD_DIM, HEAD_DIM), HEAD_DIM)
        for src, dst in ((dq_h, dq), (dk_h, dk), (dv_h, dv)):
            for k in range(SEQ):
                piece = src.at[j, lanes(seq_peer[k][1], TOK), :]
                if k == 0:
                    moves.local(piece, dst.at[:, own_cols])
                else:
                    moves.remote(piece, dst.at[:, own_cols], seq_peer[k])

    out_copies = []

    def own_rows(cols):
        return part[x, :, cols].astype(F32) + rs_rx[0, :, cols].astype(F32) + rs_rx[1, :, cols].astype(F32)

    def out_send(n):
        cols = pl.ds(n * 1024, 1024)
        moves.arrive(*rs_copies[2 * n:2 * n + 2])

        @pl.when(b == 1)
        def _():
            rounded = own_rows(cols).astype(BF16)
            out_tx[:, cols] = rounded
            out[:, cols] = rounded

        out_copies.append(
            moves.remote(out_tx.at[:, cols], out_rx.at[:, cols], branch_peer, sender=1, receiver=0)
        )

    backward_head(0)

    moves.arrive(wg_swap)

    @pl.when(b == 1)
    def _():
        wg_z[...] = (wg_own[...] + wg_rx[...].astype(F32)).astype(BF16)

    def z_send(slot, group, k_right, k_left):
        return [
            moves.remote(wg_z.at[group[0], unit(k_right), :], wg_zrx.at[0, slot, group[0]], z_right, 1, 1),
            moves.remote(wg_z.at[group[1], unit(k_left), :], wg_zrx.at[1, slot, group[1]], z_left, 1, 1),
        ]

    both = pl.ds(0, 2)
    z_moves = z_send(0, (0, 1), 4, 4)

    def z_step(t):
        nonlocal z_moves
        moves.arrive(*z_moves)
        groups = (0, 1) if t == 1 else (both, both)

        @pl.when(b == 1)
        def _():
            for way, at in ((0, unit(4 - t)), (1, unit(4 + t))):
                wg_z[groups[way], at, :] = (
                    wg_z[groups[way], at, :].astype(F32) + wg_zrx[way, t - 1, groups[way]].astype(F32)
                ).astype(BF16)

        z_moves = z_send(t, (both, both), 4 - t, 4 + t)

    out_send(0)
    backward_head(1)
    z_step(1)
    out_send(1)
    backward_head(2)
    out_send(2)

    z_step(2)
    z_step(3)
    moves.arrive(*z_moves)

    @pl.when(b == 1)
    def _():
        summed = wg_z[:, unit(0), :].astype(F32)
        summed += wg_zrx[0, 3].astype(F32) + wg_zrx[1, 3].astype(F32)
        wg_acc[...] = summed * (1.0 / 16.0)

    wg_y = moves.remote(wg_acc.at[1 - h], wg_yrx, y_peer, sender=1, receiver=1)
    moves.arrive(wg_y)

    @pl.when(b == 1)
    def _():
        wg_tot[...] = wg_acc[h] + wg_yrx[...]

    away = pl.ds(pl.multiple_of((1 - c) * ROWS, 8), ROWS)
    wg_c = moves.remote(wg_tot.at[away, :], wg_crx, core_peer, sender=1, receiver=1)
    moves.arrive(wg_c)

    @pl.when(b == 1)
    def _():
        wg[:, own_half] = wg_tot[pl.ds(pl.multiple_of(c * ROWS, 8), ROWS), :]
        wg[:, other_half] = wg_crx[...]

    moves.arrive(*out_copies)

    @pl.when(b == 0)
    def _():
        out[...] = (own_rows(slice(None)) + out_rx[...].astype(F32)).astype(BF16)
        wg[...] = jnp.zeros((ROWS, WIDTH), F32)

    moves.finish()


def settle_kernel(*refs):
    for source, target in zip(refs[:5], refs[5:]):
        target[...] = source[...]


def settle(*arrays):
    specs = [pl.BlockSpec((TOK // 4, WIDTH), lambda i: (i, 0))] * 4
    specs.append(pl.BlockSpec((ROWS // 3, WIDTH), lambda i: (jnp.minimum(i, 2), 0)))
    return pl.pallas_call(
        settle_kernel,
        grid=(4,),
        out_shape=tuple(jax.ShapeDtypeStruct(a.shape, a.dtype) for a in arrays),
        in_specs=specs,
        out_specs=tuple(specs),
        compiler_params=pltpu.CompilerParams(vmem_limit_bytes=60 * 2**20),
        name="settle",
    )(*arrays)


def vmem(shape, dtype=BF16):
    return pltpu.VMEM(shape, dtype)


def time_features(step_value, feature_count):
    half_count = feature_count // 2
    frequency = jnp.exp(-math.log(10000.0) * jnp.arange(half_count, dtype=F32) / half_count)
    phases = step_value.astype(F32) * frequency
    raw_features = jnp.concatenate([jnp.cos(phases), jnp.sin(phases)])
    return jax.nn.silu(raw_features).astype(BF16)


def shards(
    query_rows, key_rows, value_rows, cotangent, proj_weight, time_weight, timestep, text_count
):
    features = time_features(timestep[0], time_weight.shape[1])
    gate_row = jnp.dot(features[None, :], time_weight[0], preferred_element_type=F32)
    bias = jnp.where(jnp.arange(TEXT) < text_count[0], 0.0, -jnp.inf).astype(F32)[None, :]
    any_spec = pl.BlockSpec(memory_space=pl.ANY)
    vmem_spec = pl.BlockSpec(memory_space=pltpu.VMEM)
    rows_shape = jax.ShapeDtypeStruct((TOK, WIDTH), BF16)
    scratch = [
        vmem((HEADS, LENGTH, HEAD_DIM)), vmem((HEADS, LENGTH, HEAD_DIM)),
        vmem((HEADS, LENGTH, 2 * HEAD_DIM)),
        vmem((HEADS, LENGTH, LENGTH)),
        vmem((HEADS, LENGTH, HEAD_DIM), F32), vmem((HEADS, LENGTH, HEAD_DIM), F32),
        vmem((4, 2, TOK, GROUP)), vmem((2, 4, TOK, GROUP)),
        vmem((4, TOK, WIDTH)), vmem((4, 2, TOK, GROUP)), vmem((2, 4, TOK, GROUP)),
        vmem((LENGTH, HEAD_DIM)), vmem((LENGTH, LENGTH)),
        vmem((HEADS, LENGTH, HEAD_DIM)), vmem((HEADS, LENGTH, HEAD_DIM)),
        vmem((HEADS, LENGTH, HEAD_DIM)),
        vmem((ROWS, WIDTH), F32), vmem((ROWS, HALF), F32), vmem((2, GROUP, WIDTH)),
        vmem((TOK, WIDTH)), vmem((4, TOK, WIDTH)), vmem((2, 64, WIDTH)), vmem((2, TOK, WIDTH)),
        vmem((TOK, WIDTH)), vmem((TOK, WIDTH)),
        vmem((2, GROUP, HALF), F32), vmem((2, GROUP, HALF)), vmem((2, GROUP, HALF)),
        vmem((2, GROUP, HALF)), vmem((2, 4, 2, UNIT, HALF)),
        vmem((2, UNIT, HALF), F32), vmem((UNIT, HALF), F32), vmem((UNIT, HALF), F32),
        vmem((ROWS, HALF), F32),
        pltpu.SemaphoreType.DMA((COPIES,)), pltpu.SemaphoreType.DMA((COPIES,)),
        pltpu.SemaphoreType.DMA((32,)),
    ]
    block_out, dq, dk, dv, wg = pl.pallas_call(
        kernel,
        out_shape=(rows_shape, rows_shape, rows_shape, rows_shape,
                   jax.ShapeDtypeStruct((ROWS, WIDTH), F32)),
        in_specs=[any_spec] * 3 + [vmem_spec] * 4,
        out_specs=(vmem_spec, any_spec, any_spec, any_spec, vmem_spec),
        scratch_shapes=scratch,
        compiler_params=pltpu.CompilerParams(
            collective_id=0, has_side_effects=True, vmem_limit_bytes=60 * 2**20
        ),
        cost_estimate=pl.CostEstimate(
            flops=14 * 10**9, bytes_accessed=8 * 10**6, transcendentals=3 * 2**20
        ),
        name="block",
    )(query_rows[0, 0], key_rows[0, 0], value_rows[0, 0], cotangent[0, 0], proj_weight[0],
      gate_row, bias)
    results = settle(block_out, dq, dk, dv, wg)
    return tuple(rows[None, None] for rows in results[:4]) + (results[4][None],)


def solution(mesh):
    rows = P("branch", "dp", "seq", None)
    weight = P("branch", ("seq", "dp"), None)
    return jax.shard_map(
        shards,
        mesh=mesh,
        in_specs=(rows, rows, rows, rows, weight, P("branch", None, None), P("dp"), P("dp")),
        out_specs=(rows, rows, rows, rows, weight),
        check_vma=False,
    )
```

```python
import functools
import math

import jax
import jax.numpy as jnp
from jax import lax
from jax.experimental import pallas as pl
from jax.experimental.pallas import tpu as pltpu
from jax.sharding import PartitionSpec as P

HEAD_DIM = 128
TOK = 128
SEQ = 8
WIDTH = 3072
GROUP = 384
HEADS = 3
LENGTH = 1024
TEXT = 256
HALF = 1536
UNIT = 48
ROWS = 24
MESH = pl.DeviceIdType.MESH
F32 = jnp.float32
BF16 = jnp.bfloat16
SCALE = HEAD_DIM ** (-0.5)
TO_EXP2 = SCALE * math.log2(math.e)
COPIES = 192


def dot(a, b):
    return jnp.dot(a, b, preferred_element_type=F32)


def dot_rows(a, b):
    return lax.dot_general(a, b, (((1,), (1,)), ((), ())), preferred_element_type=F32)


class Transfers:
    def __init__(self, branch, send_sem, recv_sem, local_sem):
        self.branch, self.sems, self.local_sem = branch, (send_sem, recv_sem), local_sem
        self.remotes, self.locals = 0, 0
        self.sends, self.recvs = [], []

    def on(self, side, action):
        if side is None:
            action()
        else:
            pl.when(self.branch == side)(action)

    def remote(self, src, dst, device, sender=None, receiver=None):
        i = self.remotes
        self.remotes += 1
        copy = pltpu.make_async_remote_copy(
            src_ref=src, dst_ref=dst, send_sem=self.sems[0].at[i], recv_sem=self.sems[1].at[i],
            device_id=device, device_id_type=MESH,
        )
        self.on(sender, copy.start)
        self.sends.append((copy, sender))
        self.recvs.append((copy, receiver, True))
        return copy

    def local(self, src, dst):
        i = self.locals
        self.locals += 1
        copy = pltpu.make_async_copy(src, dst, self.local_sem.at[i])
        copy.start()
        self.recvs.append((copy, None, False))
        return copy

    def arrive(self, *copies):
        for copy in copies:
            entry = next(e for e in self.recvs if e[0] is copy)
            self.recvs = [e for e in self.recvs if e is not entry]
            self.on(entry[1], copy.wait_recv if entry[2] else copy.wait)

    def sent(self, copy):
        entry = next(e for e in self.sends if e[0] is copy)
        self.sends = [e for e in self.sends if e is not entry]
        self.on(entry[1], copy.wait_send)

    def finish(self):
        self.arrive(*[entry[0] for entry in self.recvs])
        for copy, side in self.sends:
            self.on(side, copy.wait_send)


def kernel(
    q_in, k_in, v_in, cot_in, w_in, gate_in, bias_in,
    out, dq, dk, dv, wg,
    q_h, k_h, v_h, exps, o_f, l_inv, att, att2, g_tok, g_h, ag, gs_buf, ds_buf,
    dq_h, dk_h, dv_h, w_own, w_rx, w_all, cot_rx, part, rs_relay, rs_rx, out_tx, out_rx,
    wg_own, wg_tx, wg_rx, wg_z, wg_zrx, wg_acc, wg_yrx, wg_tot, wg_crx,
    send_sem, recv_sem, local_sem,
):
    b = lax.axis_index("branch")
    s = lax.axis_index("seq")
    d = lax.axis_index("dp")
    x, h = lax.div(s, 2), lax.rem(s, 2)
    z, c = lax.div(d, 2), lax.rem(d, 2)
    seq_peer = [(b, lax.rem(s + k, SEQ), d) for k in range(SEQ)]
    z_peer = [(b, s, lax.rem(d + 2 * k, 16)) for k in range(8)]
    x_right, x_left = seq_peer[2], seq_peer[6]
    z_right, z_left = z_peer[1], z_peer[7]
    y_peer = (b, s + 1 - 2 * h, d)
    core_peer = (b, s, d + 1 - 2 * c)
    branch_peer = (1 - b, s, d)
    moves = Transfers(b, send_sem, recv_sem, local_sem)

    barrier = pltpu.get_barrier_semaphore()
    everyone = seq_peer[1:] + z_peer[1:] + [core_peer, branch_peer]
    for device in everyone:
        pl.semaphore_signal(barrier, inc=1, device_id=device, device_id_type=MESH)
    w_own[...] = w_in[...].astype(F32)
    v_h[:, :, HEAD_DIM:] = jnp.ones((HEADS, LENGTH, HEAD_DIM), BF16)
    pl.semaphore_wait(barrier, len(everyone))

    def lanes(index, size):
        return pl.ds(pl.multiple_of(index * size, size), size)

    own_half = lanes(c, HALF)
    other_half = lanes(1 - c, HALF)

    def unit(k):
        return pl.ds(pl.multiple_of(lax.rem(z + k + 8, 8) * UNIT, 16), UNIT)

    w_copy = moves.remote(w_own.at[:, other_half], w_rx, core_peer)
    top, low = pl.ds(0, 64), pl.ds(64, 64)
    cot_copies = [
        moves.remote(cot_in.at[rows], cot_rx.at[rows], branch_peer, sender=0, receiver=1)
        for rows in (top, low)
    ]

    def send_in(j, offsets):
        copies = []
        for src, dst, wide in ((q_in, q_h, False), (k_in, k_h, False), (v_in, v_h, True)):
            here = dst.at[j, lanes(s, TOK), pl.ds(0, HEAD_DIM)] if wide else dst.at[j, lanes(s, TOK), :]
            for k in offsets:
                peer = seq_peer[k][1]
                cols = pl.ds(pl.multiple_of(peer * GROUP + j * HEAD_DIM, HEAD_DIM), HEAD_DIM)
                if k == 0:
                    copies.append(moves.local(src.at[:, cols], here))
                else:
                    copies.append(moves.remote(src.at[:, cols], here, seq_peer[k]))
        return copies

    moves.arrive(w_copy)
    first = c == 0
    own_part = w_own[:, own_half]
    other_part = w_rx[...]
    w_all[h, unit(0), own_half] = jnp.concatenate(
        [jnp.where(first, own_part, other_part), jnp.where(first, other_part, own_part)], axis=0
    ).astype(BF16)
    w_y = moves.remote(w_all.at[h, unit(0), own_half], w_all.at[h, unit(0), own_half], y_peer)
    in_copies = [send_in(j, (0, 2, 6, 4)) for j in range(HEADS)]
    moves.arrive(w_y)
    w_swaps = []

    def w_swap(k):
        piece = w_all.at[:, unit(k), own_half]
        w_swaps.append(moves.remote(piece, piece, core_peer))

    def w_send(k, peer):
        piece = w_all.at[:, unit(k), own_half]
        return moves.remote(piece, piece, peer)

    w_moves = [w_send(0, z_right), w_send(0, z_left)]
    w_swap(0)

    def w_step(t):
        nonlocal w_moves
        moves.arrive(*w_moves)
        if t < 3:
            w_moves = [w_send(-t, z_right), w_send(t, z_left)]
        elif t == 3:
            low = w_all.at[0, unit(-3), own_half]
            high = w_all.at[1, unit(3), own_half]
            w_moves = [moves.remote(low, low, z_right), moves.remote(high, high, z_left)]
        if t < 4:
            w_swap(-t)
            w_swap(t)
        else:
            w_swap(4)

    def forward_head(j):
        moves.arrive(*in_copies[j])
        cols = slice(j * HEAD_DIM, (j + 1) * HEAD_DIM)
        for i in range(4):
            rows = pl.ds(i * 256, 256)
            queries = q_h[j, rows, :]
            text = dot_rows(queries, k_h[j, :TEXT, :]) + bias_in[...]
            image = dot_rows(queries, k_h[j, TEXT:, :])
            highest = jnp.maximum(
                jnp.max(text, axis=1, keepdims=True), jnp.max(image, axis=1, keepdims=True)
            )
            text = jnp.exp2((text - highest) * TO_EXP2).astype(BF16)
            image = jnp.exp2((image - highest) * TO_EXP2).astype(BF16)
            exps[j, rows, :TEXT] = text
            exps[j, rows, TEXT:] = image
            mixed = dot(text, v_h[j, :TEXT, :]) + dot(image, v_h[j, TEXT:, :])
            inverse = 1.0 / mixed[:, HEAD_DIM:]
            result = mixed[:, :HEAD_DIM] * inverse
            l_inv[j, rows, :] = inverse
            o_f[j, rows, :] = result
            result = result.astype(BF16)
            att[i, 0, :, cols] = result[:TOK]
            att[i, 1, :, cols] = result[TOK:]
        cols = pl.ds(j * HEAD_DIM, HEAD_DIM)
        return [
            moves.remote(att.at[:, 1 - h, :, cols], att2.at[h, :, :, cols], y_peer),
            moves.local(att.at[:, h, :, cols], att2.at[h, :, :, cols]),
        ]

    def gate_rows(rows):
        @pl.when(b == 0)
        def _():
            g_tok[x, rows] = (cot_in[rows, :].astype(F32) * gate_in[...]).astype(BF16)

        @pl.when(b == 1)
        def _():
            g_tok[x, rows] = (
                (cot_in[rows, :].astype(F32) + cot_rx[rows, :].astype(F32)) * gate_in[...]
            ).astype(BF16)

    def g_send(block, rows, peer):
        piece = g_tok.at[lax.rem(x + block, 4), rows]
        return moves.remote(piece, piece, peer)

    moves.arrive(cot_copies[0])
    gate_rows(top)
    g_first = [g_send(0, top, x_right)]
    g_rest = [g_send(0, top, x_left)]
    w_step(1)
    moves.arrive(cot_copies[1])
    gate_rows(low)
    g_first.append(g_send(0, low, x_left))
    g_rest.append(g_send(0, low, x_right))
    for copy in cot_copies:
        moves.sent(copy)
    for j in range(HEADS):
        in_copies[j] += send_in(j, (1, 7, 3, 5))
    w_step(2)
    w_step(3)
    w_step(4)
    moves.arrive(*g_first)
    g_far = [g_send(3, top, x_right), g_send(1, low, x_left)]
    att_copies = forward_head(0) + forward_head(1) + forward_head(2)
    moves.arrive(*w_swaps)

    moves.arrive(*g_rest)
    moves.arrive(*g_far)

    def attended_grad(group, i):
        rows = g_tok[pl.ds(i * 2, 2)].reshape(256, WIDTH)
        grads = dot_rows(rows, w_all[group]).astype(BF16)
        ag[group, pl.ds(i * 2, 2)] = grads.reshape(2, TOK, GROUP)

    grad_copies = [[], []]
    for i in range(2):
        attended_grad(1 - h, i)
        pair = pl.ds(i * 2, 2)
        grad_copies[i].append(moves.remote(ag.at[1 - h, pair], g_h.at[pair, h], y_peer))
    for i in range(2):
        attended_grad(h, i)
        pair = pl.ds(i * 2, 2)
        grad_copies[i].append(moves.local(ag.at[h, pair], g_h.at[pair, h]))

    moves.arrive(*att_copies)

    far, right, left = lax.rem(x + 2, 4), lax.rem(x + 1, 4), lax.rem(x + 3, 4)
    relays = []
    for n in range(3):
        cols = pl.ds(n * 1024, 1024)
        for m in range(2):
            at = pl.ds(n * 1024 + m * 512, 512)
            rows0 = att2[0].reshape(512, GROUP)
            rows1 = att2[1].reshape(512, GROUP)
            summed = dot(rows0, w_all[0, :, at]) + dot(rows1, w_all[1, :, at])
            part[:, :, at] = (summed * gate_in[:, at]).astype(BF16).reshape(4, TOK, 512)
        relays.append([
            moves.remote(part.at[far, top, cols], rs_relay.at[0, :, cols], x_right),
            moves.remote(part.at[far, low, cols], rs_relay.at[1, :, cols], x_left),
        ])

    def weight_products(half, store):
        for group in range(2):
            turned = jnp.transpose(att2[group].reshape(512, GROUP))

            def step(m, carry):
                source = pl.ds(pl.multiple_of(half * HALF + m * 512, 512), 512)
                cols = pl.ds(pl.multiple_of(m * 512, 512), 512)
                store(group, cols, dot(turned, g_tok[:, :, source].reshape(512, 512)))
                return carry

            lax.fori_loop(0, 3, step, 0)

    def store_tx(group, cols, value):
        wg_tx[group, :, cols] = value.astype(BF16)

    def store_own(group, cols, value):
        wg_own[group, :, cols] = value

    pl.when(b == 1)(lambda: weight_products(1 - c, store_tx))
    wg_swap = moves.remote(wg_tx, wg_rx, core_peer, sender=1, receiver=1)
    pl.when(b == 1)(lambda: weight_products(c, store_own))

    rs_copies = []
    for n in range(3):
        cols = pl.ds(n * 1024, 1024)
        moves.arrive(*relays[n])
        part[right, top, cols] = (
            part[right, top, cols].astype(F32) + rs_relay[0, :, cols].astype(F32)
        ).astype(BF16)
        part[left, low, cols] = (
            part[left, low, cols].astype(F32) + rs_relay[1, :, cols].astype(F32)
        ).astype(BF16)
        rs_copies += [
            moves.remote(part.at[right, :, cols], rs_rx.at[0, :, cols], x_right),
            moves.remote(part.at[left, :, cols], rs_rx.at[1, :, cols], x_left),
        ]

    def backward_head(j):
        cols = slice(j * HEAD_DIM, (j + 1) * HEAD_DIM)
        for i in range(4):
            if j == 0 and i % 2 == 0:
                moves.arrive(*grad_copies[i // 2])
            rows = pl.ds(i * 256, 256)
            grads = g_h[i, :, :, cols].reshape(256, HEAD_DIM).astype(F32)
            scaled = (grads * l_inv[j, rows, :]).astype(BF16)
            gs_buf[rows, :] = scaled
            shift = jnp.sum(scaled.astype(F32) * o_f[j, rows, :], axis=1, keepdims=True)
            prob_grad = dot_rows(scaled, v_h[j, :, :HEAD_DIM])
            score = (exps[j, rows, :].astype(F32) * (prob_grad - shift)).astype(BF16)
            ds_buf[rows, :] = score
            dq_h[j, rows, :] = (dot(score, k_h[j]) * SCALE).astype(BF16)
        q_turned = jnp.transpose(q_h[j])
        g_turned = jnp.transpose(gs_buf[...])
        for i in range(4):
            rows = pl.ds(i * 256, 256)
            key_part = dot(q_turned, ds_buf[:, rows])
            dk_h[j, rows, :] = (jnp.transpose(key_part) * SCALE).astype(BF16)
            value_part = dot(g_turned, exps[j, :, rows])
            dv_h[j, rows, :] = jnp.transpose(value_part).astype(BF16)
        own_cols = pl.ds(pl.multiple_of(s * GROUP + j * HEAD_DIM, HEAD_DIM), HEAD_DIM)
        for src, dst in ((dq_h, dq), (dk_h, dk), (dv_h, dv)):
            for k in (0, 1, 7, 3, 5, 2, 6, 4):
                piece = src.at[j, lanes(seq_peer[k][1], TOK), :]
                if k == 0:
                    moves.local(piece, dst.at[:, own_cols])
                else:
                    moves.remote(piece, dst.at[:, own_cols], seq_peer[k])

    out_copies = []

    def own_rows(cols):
        return part[x, :, cols].astype(F32) + rs_rx[0, :, cols].astype(F32) + rs_rx[1, :, cols].astype(F32)

    def out_send(n):
        cols = pl.ds(n * 1024, 1024)
        moves.arrive(*rs_copies[2 * n:2 * n + 2])

        @pl.when(b == 1)
        def _():
            rounded = own_rows(cols).astype(BF16)
            out_tx[:, cols] = rounded
            out[:, cols] = rounded

        out_copies.append(
            moves.remote(out_tx.at[:, cols], out_rx.at[:, cols], branch_peer, sender=1, receiver=0)
        )

    backward_head(0)

    moves.arrive(wg_swap)

    @pl.when(b == 1)
    def _():
        wg_z[...] = (wg_own[...] + wg_rx[...].astype(F32)).astype(BF16)

    def z_send(slot, group, k_right, k_left):
        return [
            moves.remote(wg_z.at[group[0], unit(k_right), :], wg_zrx.at[0, slot, group[0]], z_right, 1, 1),
            moves.remote(wg_z.at[group[1], unit(k_left), :], wg_zrx.at[1, slot, group[1]], z_left, 1, 1),
        ]

    both = pl.ds(0, 2)
    z_moves = z_send(0, (0, 1), 4, 4)

    def z_step(t):
        nonlocal z_moves
        moves.arrive(*z_moves)
        groups = (0, 1) if t == 1 else (both, both)

        @pl.when(b == 1)
        def _():
            for way, at in ((0, unit(4 - t)), (1, unit(4 + t))):
                wg_z[groups[way], at, :] = (
                    wg_z[groups[way], at, :].astype(F32) + wg_zrx[way, t - 1, groups[way]].astype(F32)
                ).astype(BF16)

        z_moves = z_send(t, (both, both), 4 - t, 4 + t)

    out_send(0)
    backward_head(1)
    z_step(1)
    out_send(1)
    backward_head(2)
    out_send(2)

    z_step(2)
    z_step(3)
    moves.arrive(*z_moves)

    @pl.when(b == 1)
    def _():
        summed = wg_z[:, unit(0), :].astype(F32)
        summed += wg_zrx[0, 3].astype(F32) + wg_zrx[1, 3].astype(F32)
        wg_acc[...] = summed * (1.0 / 16.0)

    wg_y = moves.remote(wg_acc.at[1 - h], wg_yrx, y_peer, sender=1, receiver=1)
    moves.arrive(wg_y)

    @pl.when(b == 1)
    def _():
        wg_tot[...] = wg_acc[h] + wg_yrx[...]

    away = pl.ds(pl.multiple_of((1 - c) * ROWS, 8), ROWS)
    wg_c = moves.remote(wg_tot.at[away, :], wg_crx, core_peer, sender=1, receiver=1)
    moves.arrive(wg_c)

    @pl.when(b == 1)
    def _():
        wg[:, own_half] = wg_tot[pl.ds(pl.multiple_of(c * ROWS, 8), ROWS), :]
        wg[:, other_half] = wg_crx[...]

    moves.arrive(*out_copies)

    @pl.when(b == 0)
    def _():
        out[...] = (own_rows(slice(None)) + out_rx[...].astype(F32)).astype(BF16)
        wg[...] = jnp.zeros((ROWS, WIDTH), F32)

    moves.finish()


def settle_kernel(*refs):
    for source, target in zip(refs[:5], refs[5:]):
        target[...] = source[...]


def settle(*arrays):
    specs = [pl.BlockSpec((TOK // 4, WIDTH), lambda i: (i, 0))] * 4
    specs.append(pl.BlockSpec((ROWS // 3, WIDTH), lambda i: (jnp.minimum(i, 2), 0)))
    return pl.pallas_call(
        settle_kernel,
        grid=(4,),
        out_shape=tuple(jax.ShapeDtypeStruct(a.shape, a.dtype) for a in arrays),
        in_specs=specs,
        out_specs=tuple(specs),
        compiler_params=pltpu.CompilerParams(vmem_limit_bytes=60 * 2**20),
        name="settle",
    )(*arrays)


def vmem(shape, dtype=BF16):
    return pltpu.VMEM(shape, dtype)


def time_features(step_value, feature_count):
    half_count = feature_count // 2
    frequency = jnp.exp(-math.log(10000.0) * jnp.arange(half_count, dtype=F32) / half_count)
    phases = step_value.astype(F32) * frequency
    raw_features = jnp.concatenate([jnp.cos(phases), jnp.sin(phases)])
    return jax.nn.silu(raw_features).astype(BF16)


def shards(
    query_rows, key_rows, value_rows, cotangent, proj_weight, time_weight, timestep, text_count
):
    features = time_features(timestep[0], time_weight.shape[1])
    gate_row = jnp.dot(features[None, :], time_weight[0], preferred_element_type=F32)
    bias = jnp.where(jnp.arange(TEXT) < text_count[0], 0.0, -jnp.inf).astype(F32)[None, :]
    any_spec = pl.BlockSpec(memory_space=pl.ANY)
    vmem_spec = pl.BlockSpec(memory_space=pltpu.VMEM)
    rows_shape = jax.ShapeDtypeStruct((TOK, WIDTH), BF16)
    scratch = [
        vmem((HEADS, LENGTH, HEAD_DIM)), vmem((HEADS, LENGTH, HEAD_DIM)),
        vmem((HEADS, LENGTH, 2 * HEAD_DIM)),
        vmem((HEADS, LENGTH, LENGTH)),
        vmem((HEADS, LENGTH, HEAD_DIM), F32), vmem((HEADS, LENGTH, HEAD_DIM), F32),
        vmem((4, 2, TOK, GROUP)), vmem((2, 4, TOK, GROUP)),
        vmem((4, TOK, WIDTH)), vmem((4, 2, TOK, GROUP)), vmem((2, 4, TOK, GROUP)),
        vmem((LENGTH, HEAD_DIM)), vmem((LENGTH, LENGTH)),
        vmem((HEADS, LENGTH, HEAD_DIM)), vmem((HEADS, LENGTH, HEAD_DIM)),
        vmem((HEADS, LENGTH, HEAD_DIM)),
        vmem((ROWS, WIDTH), F32), vmem((ROWS, HALF), F32), vmem((2, GROUP, WIDTH)),
        vmem((TOK, WIDTH)), vmem((4, TOK, WIDTH)), vmem((2, 64, WIDTH)), vmem((2, TOK, WIDTH)),
        vmem((TOK, WIDTH)), vmem((TOK, WIDTH)),
        vmem((2, GROUP, HALF), F32), vmem((2, GROUP, HALF)), vmem((2, GROUP, HALF)),
        vmem((2, GROUP, HALF)), vmem((2, 4, 2, UNIT, HALF)),
        vmem((2, UNIT, HALF), F32), vmem((UNIT, HALF), F32), vmem((UNIT, HALF), F32),
        vmem((ROWS, HALF), F32),
        pltpu.SemaphoreType.DMA((COPIES,)), pltpu.SemaphoreType.DMA((COPIES,)),
        pltpu.SemaphoreType.DMA((32,)),
    ]
    block_out, dq, dk, dv, wg = pl.pallas_call(
        kernel,
        out_shape=(rows_shape, rows_shape, rows_shape, rows_shape,
                   jax.ShapeDtypeStruct((ROWS, WIDTH), F32)),
        in_specs=[any_spec] * 3 + [vmem_spec] * 4,
        out_specs=(vmem_spec, any_spec, any_spec, any_spec, vmem_spec),
        scratch_shapes=scratch,
        compiler_params=pltpu.CompilerParams(
            collective_id=0, has_side_effects=True, vmem_limit_bytes=60 * 2**20
        ),
        cost_estimate=pl.CostEstimate(
            flops=14 * 10**9, bytes_accessed=8 * 10**6, transcendentals=3 * 2**20
        ),
        name="block",
    )(query_rows[0, 0], key_rows[0, 0], value_rows[0, 0], cotangent[0, 0], proj_weight[0],
      gate_row, bias)
    results = settle(block_out, dq, dk, dv, wg)
    return tuple(rows[None, None] for rows in results[:4]) + (results[4][None],)


def solution(mesh):
    rows = P("branch", "dp", "seq", None)
    weight = P("branch", ("seq", "dp"), None)
    return jax.shard_map(
        shards,
        mesh=mesh,
        in_specs=(rows, rows, rows, rows, weight, P("branch", None, None), P("dp"), P("dp")),
        out_specs=(rows, rows, rows, rows, weight),
        check_vma=False,
    )
```
